32 devices in a mesh: tgt: 16 (over z, y, core), src: 2 (over x).
Axes of the slice: x: 2, y: 2, z: 4, core: 2. Of those that a mesh axis runs over, the one named last changes fastest.
Arguments:
- tgt_points: bfloat16 [3, 8192], P(None, 'tgt'), may hold values from -4 to 4
- tgt_weight: float32 [8192], P('tgt'), may hold values from 0.5 to 2
- src_points: bfloat16 [4, 3, 4096], P(None, None, ('tgt', 'src')), may hold values from -4 to 4
- src_weight: float32 [4, 4096], P(None, ('tgt', 'src')), may hold values from 0.5 to 2
- basis: float32 [4, 3, 4096], P(None, None, ('tgt', 'src')), may hold values from 0.05 to 1
- span: int32 [4, 4096], P(None, ('tgt', 'src')), may hold values from 0 to 29
- patch: int32 [4, 4096], P(None, ('tgt', 'src')), may hold values from 0 to 3
- patch_factor: float32 [4, 2, 128], P(None, None, ('tgt', 'src')), may hold values from -1.5 to 1.5
- ctrl_weight: float32 [4, 1024], P(None, ('tgt', 'src')), may hold values from 0.5 to 2
- ctrl_coef: bfloat16 [4, 128, 1024], P(None, None, ('tgt', 'src')), may hold values from -6 to 6
- band: float32 [8, 8192], P(None, 'tgt'), may hold values from -0.5 to 0.5
- offsets: int32 [8], replicated, may hold values from -8 to 8, as said below
Outputs:
- shell_field: float32 [8192, 128], P('tgt')
The draws below stay inside these ranges and needn't reach their ends.
Inputs may be any that keep to these rules, and one draw needn't show every extreme that they name: span of source point j is local to the 32 control points of the block j // 128. patch of source point j is local to the 4 patches of the block j // 128. offsets[0] is 8 and offsets[1] is -8.
All inputs are finite; a program needn't handle non-finite values.
Results may differ from the reference program's by a relative error of at most 0.0041.
Values may be sent and summed in bfloat16 or wider, within the bound.
A program may use at most 128 MiB of HBM per device.

```python
import math
import jax
import jax.numpy as jnp
from jax import lax

SRC_DEV = 128
ROUNDS = 4
NRHS = 64
DEGREE = 2
PATCH_DEV = 4
HALO = 8
NB = 8
ORDER = 3
CTRL_DEV = 32
TARGETS = 8192
SOURCES = 4096
CONTROLS = 1024
PATCHES = 128


def draw_offsets(key, part):
    values = jax.random.randint(key, (NB,), -HALO, HALO + 1)
    values = values.at[0].set(HALO).at[1].set(-HALO)
    return values.astype(jnp.int32)


def touch_ends(array, rng, least, high):
    shape = array.shape
    place = [jax.random.randint(jax.random.fold_in(rng, axis), (), 0, shape[axis]) for axis in range(len(shape))]
    array = array.at[tuple(place)].set(least)
    longest = shape.index(max(shape))
    place[longest] = (place[longest] + 1) % shape[longest]
    return array.at[tuple(place)].set(high)


def steps_of(key, extent, pieces, smallest, top_value):
    factor_of = 1.0
    for axis_at, shards_of in pieces:
        draws = jax.random.uniform(jax.random.fold_in(jax.random.fold_in(key, 6), axis_at), (shards_of,), jnp.float32, smallest / len(pieces), top_value / len(pieces))
        factor_of = factor_of * jnp.repeat(jnp.exp(draws), extent[axis_at] // shards_of).reshape((-1,) + (1,) * (len(extent) - 1 - axis_at))
    return factor_of


def scatter_about(own_key, extent, width, bound, split=(), held_as=jnp.bfloat16):
    gain = steps_of(own_key, extent, split, -0.22, 0.18) if split else 1.0
    result = jax.random.normal(own_key, extent, jnp.float32) * width * gain
    return jnp.minimum(jnp.maximum(result, -bound), bound).astype(held_as)


def setup_inputs(seed: int = 0) -> dict:
    arg_keys = jax.random.split(jax.random.key(seed), 13)
    tgt_points = scatter_about(arg_keys[0], (3, TARGETS), 1.0, 4.0, ((1, 16),))
    tgt_weight = jnp.clip(jnp.exp(math.log(2.0) - 1.3862944 * jax.random.uniform(arg_keys[1], (TARGETS,), jnp.float32) ** steps_of(arg_keys[1], (TARGETS,), ((0, 16),), -0.2, 0.2)), 0.5, 2.0)
    src_points = scatter_about(arg_keys[2], (ROUNDS, 3, SOURCES), 1.0, 4.0, ((2, 32),))
    src_weight = jnp.clip(jnp.exp(math.log(2.0) - 1.3862944 * jax.random.uniform(arg_keys[3], (ROUNDS, SOURCES), jnp.float32) ** steps_of(arg_keys[3], (ROUNDS, SOURCES), ((1, 32),), -0.2, 0.2)), 0.5, 2.0)
    basis = jnp.clip(0.05 + 0.95 * jax.random.uniform(arg_keys[4], (ROUNDS, ORDER, SOURCES), jnp.float32) ** steps_of(arg_keys[4], (ROUNDS, ORDER, SOURCES), ((2, 32),), -0.2, 0.2), 0.05, 1.0)
    span = touch_ends(jax.random.randint(arg_keys[5], (ROUNDS, SOURCES), 0, CTRL_DEV - DEGREE), jax.random.fold_in(arg_keys[5], 1), 0, (CTRL_DEV - DEGREE) - 1).astype(jnp.int32)
    patch = touch_ends(jax.random.randint(arg_keys[6], (ROUNDS, SOURCES), 0, PATCH_DEV), jax.random.fold_in(arg_keys[6], 1), 0, PATCH_DEV - 1).astype(jnp.int32)
    patch_factor = jnp.clip(jax.random.uniform(arg_keys[7], (ROUNDS, 2, PATCHES), jnp.float32, -1.5, 1.5) * steps_of(arg_keys[7], (ROUNDS, 2, PATCHES), ((2, 32),), -0.4, 0.0), -1.5, 1.5)
    ctrl_weight = jnp.clip(jnp.exp(math.log(2.0) - 1.3862944 * jax.random.uniform(arg_keys[8], (ROUNDS, CONTROLS), jnp.float32) ** steps_of(arg_keys[8], (ROUNDS, CONTROLS), ((1, 32),), -0.2, 0.2)), 0.5, 2.0)
    ctrl_coef = scatter_about(arg_keys[9], (ROUNDS, 2 * NRHS, CONTROLS), 1.0, 6.0, ((2, 32),))
    band = jnp.clip(jax.random.uniform(arg_keys[10], (NB, TARGETS), jnp.float32, -0.5, 0.5) * steps_of(arg_keys[10], (NB, TARGETS), ((1, 16),), -0.4, 0.0), -0.5, 0.5)
    offsets = draw_offsets(jax.random.fold_in(arg_keys[12], 71), 0)
    return {"tgt_points": tgt_points, "tgt_weight": tgt_weight, "src_points": src_points, "src_weight": src_weight, "basis": basis, "span": span, "patch": patch, "patch_factor": patch_factor, "ctrl_weight": ctrl_weight, "ctrl_coef": ctrl_coef, "band": band, "offsets": offsets}


WAVE = 8.0
SMOOTH = 0.0025

def kernel_terms(targets, sources, density):
    tpos = targets.astype(jnp.float32)
    spos = sources.astype(jnp.float32)
    dist_sq = SMOOTH + (tpos[0][:, None] - spos[0][None, :]) ** 2
    dist_sq = dist_sq + (tpos[1][:, None] - spos[1][None, :]) ** 2
    dist_sq = dist_sq + (tpos[2][:, None] - spos[2][None, :]) ** 2
    dist = jnp.sqrt(dist_sq)
    kernel_re = (jnp.cos(WAVE * dist) / dist).astype(jnp.bfloat16)
    kernel_im = (jnp.sin(WAVE * dist) / dist).astype(jnp.bfloat16)
    dims = (((1,), (1,)), ((), ()))
    part_a = lax.dot_general(kernel_re.astype(jnp.float32), density.astype(jnp.float32), dims)
    part_b = lax.dot_general(kernel_im.astype(jnp.float32), density.astype(jnp.float32), dims)
    half = density.shape[0] // 2
    return jnp.concatenate([part_a[:, :half] - part_b[:, half:], part_a[:, half:] + part_b[:, :half]], axis=1)

def round_density(section, src_weight, basis, span, patch, patch_factor, ctrl_weight, ctrl_coef):
    count = src_weight.shape[1]
    block = jnp.arange(count, dtype=jnp.int32) // SRC_DEV
    base = block * CTRL_DEV + span[section]
    denom = jnp.zeros((count,), jnp.float32)
    numer = jnp.zeros((ctrl_coef.shape[1], count), jnp.float32)
    for basis_index in range(ORDER):
        control_index = (base + basis_index).astype(jnp.int32)
        scaled = basis[section, basis_index] * ctrl_weight[section][control_index]
        denom = denom + scaled
        numer = numer + scaled[None, :] * ctrl_coef[section][:, control_index].astype(jnp.float32)
    ratio = numer / denom[None, :]
    factor_index = (block * PATCH_DEV + patch[section]).astype(jnp.int32)
    factor_re = patch_factor[section, 0][factor_index]
    factor_im = patch_factor[section, 1][factor_index]
    ratio_re = ratio[:NRHS]
    ratio_im = ratio[NRHS:]
    weight = src_weight[section]
    dens_re = weight * (factor_re * ratio_re - factor_im * ratio_im)
    dens_im = weight * (factor_re * ratio_im + factor_im * ratio_re)
    return jnp.concatenate([dens_re, dens_im], axis=0).astype(jnp.bfloat16)

def reference(tgt_points, tgt_weight, src_points, src_weight, basis, span, patch, patch_factor, ctrl_weight, ctrl_coef, band, offsets):
    count = src_weight.shape[1]
    block_size = math.gcd(count, 2048)
    total = jnp.zeros((TARGETS, 2 * NRHS), jnp.float32)
    for section in range(ROUNDS):
        density = round_density(section, src_weight, basis, span, patch, patch_factor, ctrl_weight, ctrl_coef)
        sources = src_points[section]

        def step_fn(index, carried):
            start = (index * block_size).astype(jnp.int32)
            piece_src = lax.dynamic_slice_in_dim(sources, start, block_size, 1)
            piece_den = lax.dynamic_slice_in_dim(density, start, block_size, 1)
            return carried + kernel_terms(tgt_points, piece_src, piece_den)
        total = lax.fori_loop(0, count // block_size, step_fn, total)
    scale = jnp.float32(1.0 / math.sqrt(ROUNDS * SOURCES))
    potential = total * scale * tgt_weight[:, None]
    padded = jnp.pad(potential, ((HALO, HALO), (0, 0)))
    shell_field = potential
    for diag in range(NB):
        start = (HALO + offsets[diag]).astype(jnp.int32)
        rows = lax.dynamic_slice_in_dim(padded, start, TARGETS, 0)
        shell_field = shell_field + band[diag][:, None] * rows
    return shell_field
```

```python
import functools
import math

import jax
import jax.numpy as jnp
from jax import lax
from jax.experimental import pallas as pl
from jax.experimental.pallas import tpu as pltpu
from jax.sharding import PartitionSpec as P

HALO = 8
WAVE = 8.0
SMOOTH = 0.0025
OMEGA = WAVE / (2.0 * math.pi)
KAPPA = OMEGA * OMEGA
MAGIC = 12582912.0

F32 = jnp.float32
BF16 = jnp.bfloat16
MESH = pl.DeviceIdType.MESH


def pieces(value):
    high = value.astype(BF16).astype(F32)
    rest = value - high
    mid = rest.astype(BF16).astype(F32)
    return high, mid, (rest - mid).astype(BF16).astype(F32)


def flip(index, bits):
    out = index
    place = 1
    while place <= bits:
        if bits // place % 2:
            out = out + (1 - 2 * ((index // place) % 2)) * place
        place *= 2
    return out


def target_rows(points):
    square = KAPPA * (
        points[0:1] * points[0:1] + points[1:2] * points[1:2] + points[2:3] * points[2:3]
    )
    high, mid, low = pieces(square)
    one = jnp.ones_like(square)
    return jnp.concatenate(
        [points, points, points, high, mid, low, one, one, one, jnp.zeros_like(one)], axis=0
    )


def source_rows(points):
    square = KAPPA * (
        SMOOTH
        + points[0:1] * points[0:1]
        + points[1:2] * points[1:2]
        + points[2:3] * points[2:3]
    )
    high, mid, low = pieces(square)
    ph, pm, plo = pieces(points * (-2.0 * KAPPA))
    one = jnp.ones_like(square)
    return jnp.concatenate(
        [ph, pm, plo, one, one, one, high, mid, low, jnp.zeros_like(one)], axis=0
    )


SIN = (4.441527135827024, -7.264541902232219, 3.2516001820136307)
COS = (1.4133599520203266, -6.916869803046874, 5.067054327781224)


def wave_terms(square):
    inv = lax.rsqrt(square)
    turns = square * inv
    frac = turns - ((turns + MAGIC) - MAGIC)
    z = frac * frac
    half_sin = frac * (SIN[0] + z * (SIN[1] + z * SIN[2]))
    half_cos = COS[0] + z * (COS[1] + z * COS[2])
    prod = half_sin * inv
    return inv - half_sin * prod, prod * half_cos


def body(
    n_tgt,
    n_src,
    scale,
    tgt_ref,
    tw_ref,
    src_ref,
    sw_ref,
    basis_ref,
    span_ref,
    patch_ref,
    pf_ref,
    cw_ref,
    coef_ref,
    band_ref,
    off_ref,
    out_ref,
    gather,
    taug,
    bw,
    hal_own,
    hal_in,
    hw,
    saug_a,
    saug_b,
    dens_a,
    dens_b,
    kern0,
    kern1,
    kern2,
    acc,
    part,
    peers,
    pot,
    send_sem,
    recv_sem,
    hsend,
    hrecv,
    psend,
    precv,
):
    me = lax.axis_index("tgt")
    sme = lax.axis_index("src")
    rows = tgt_ref.shape[1]
    rounds, fields2, ctrl = coef_ref.shape
    half = fields2 // 2
    count = sw_ref.shape[1]
    odd = me % 2
    up = (me + 1) % n_tgt
    down = (me + n_tgt - 1) % n_tgt
    other = (me + n_tgt - 1 + 2 * odd) % n_tgt

    barrier = pltpu.get_barrier_semaphore()
    greeted = 0
    for bits in [1] + list(range(2, n_tgt, 2)):
        pl.semaphore_signal(
            barrier, inc=1, device_id=(flip(me, bits), sme), device_id_type=MESH
        )
        greeted += 1
    pl.semaphore_signal(barrier, inc=1, device_id=(other, sme), device_id_type=MESH)
    greeted += 1
    for bits in range(1, n_src):
        pl.semaphore_signal(
            barrier, inc=1, device_id=(me, flip(sme, bits)), device_id_type=MESH
        )
        greeted += 1

    gather[0, 0:fields2, :] = jnp.concatenate(
        [coef_ref[r].astype(F32) for r in range(rounds)], axis=1
    ).astype(BF16)
    for r in range(rounds):
        span = span_ref[r : r + 1, :]
        index = jnp.broadcast_to(span, (8, count)) + lax.broadcasted_iota(
            jnp.int32, (8, count), 0
        )
        weights = jnp.zeros((8, count), F32)
        for c in range(ctrl):
            weights = jnp.where(index == c, cw_ref[r, c], weights)
        scaled = basis_ref[r] * weights[0:3]
        denom = scaled[0:1] + scaled[1:2] + scaled[2:3]
        scaled = scaled * (sw_ref[r : r + 1, :] / denom)
        patch = patch_ref[r : r + 1, :]
        fre = jnp.zeros((1, count), F32)
        fim = jnp.zeros((1, count), F32)
        for p in range(pf_ref.shape[2]):
            fre = jnp.where(patch == p, pf_ref[r, 0, p], fre)
            fim = jnp.where(patch == p, pf_ref[r, 1, p], fim)
        frh, frl, _ = pieces(fre)
        fih, fil, _ = pieces(fim)
        sh, sl, _ = pieces(scaled)
        meta = jnp.concatenate(
            [
                src_ref[r].astype(F32),
                span.astype(F32),
                frh,
                frl,
                fih,
                fil,
                sh,
                sl,
                jnp.zeros((2, count), F32),
            ],
            axis=0,
        )
        gather[0, fields2 + 16 * r : fields2 + 16 * (r + 1), :] = meta.astype(BF16)

    points = tgt_ref[...].astype(F32)
    tweight = tw_ref[...]
    strip = jnp.concatenate([points, tweight, jnp.zeros((4, rows), F32)], axis=0)
    hal_own[0] = strip[:, 0:128]
    hal_own[1] = strip[:, rows - 128 : rows]

    pl.semaphore_wait(barrier, greeted)

    def direct(bits):
        return pltpu.make_async_remote_copy(
            src_ref=gather.at[0],
            dst_ref=gather.at[bits],
            send_sem=send_sem.at[bits],
            recv_sem=recv_sem.at[bits],
            device_id=(flip(me, bits), sme),
            device_id_type=MESH,
        )

    def forward(slot):
        return pltpu.make_async_remote_copy(
            src_ref=gather.at[slot],
            dst_ref=gather.at[slot + 1],
            send_sem=send_sem.at[slot + 1],
            recv_sem=recv_sem.at[slot + 1],
            device_id=(flip(me, 1), sme),
            device_id_type=MESH,
        )

    forward(0).start()
    for bits in range(2, n_tgt, 2):
        direct(bits).start()
    halo_up = pltpu.make_async_remote_copy(
        src_ref=hal_own.at[1],
        dst_ref=hal_in.at[0],
        send_sem=hsend.at[0],
        recv_sem=hrecv.at[0],
        device_id=(up, sme),
        device_id_type=MESH,
    )
    halo_down = pltpu.make_async_remote_copy(
        src_ref=hal_own.at[0],
        dst_ref=hal_in.at[1],
        send_sem=hsend.at[1],
        recv_sem=hrecv.at[1],
        device_id=(down, sme),
        device_id_type=MESH,
    )
    halo_up.start()
    halo_down.start()

    taug[0:rows, :] = jnp.transpose(target_rows(points)).astype(BF16)
    bw[...] = jnp.transpose(
        jnp.concatenate([band_ref[...], strip[3:4], jnp.zeros((7, rows), F32)], axis=0)
    )
    acc[...] = jnp.zeros_like(acc)
    halo_up.wait()
    halo_down.wait()
    low = hal_in[0]
    high = hal_in[1]
    low_t = jnp.transpose(target_rows(low[0:3]))
    high_t = jnp.transpose(target_rows(high[0:3]))
    taug[rows : rows + 16, :] = jnp.concatenate(
        [high_t[0:8], low_t[120:128]], axis=0
    ).astype(BF16)
    hw[0:8, :] = jnp.transpose(high)[0:8] * jnp.where(me < n_tgt - 1, 1.0, 0.0)
    hw[8:16, :] = jnp.transpose(low)[120:128] * jnp.where(me > 0, 1.0, 0.0)

    def prepare(slot, saug, dens):
        coef = gather[slot, 0:fields2, :]
        coef2 = jnp.concatenate([coef, coef], axis=1)
        label = lax.broadcasted_iota(jnp.int32, (ctrl, count), 0).astype(F32)
        for r in range(rounds):
            meta = gather[slot, fields2 + 16 * r : fields2 + 16 * (r + 1), :].astype(F32)
            saug[:, r * count : (r + 1) * count] = source_rows(meta[0:3]).astype(BF16)
            spread_h = jnp.zeros((ctrl, count), F32)
            spread_l = jnp.zeros((ctrl, count), F32)
            for a in range(3):
                hit = label == meta[3:4] + float(a)
                spread_h = jnp.where(hit, meta[8 + a : 9 + a], spread_h)
                spread_l = jnp.where(hit, meta[11 + a : 12 + a], spread_l)

            def placed(block):
                parts = [block.astype(BF16)]
                if r:
                    parts = [jnp.zeros((r * ctrl, count), BF16)] + parts
                if r < rounds - 1:
                    parts = parts + [jnp.zeros(((rounds - 1 - r) * ctrl, count), BF16)]
                return parts

            spread = jnp.concatenate(placed(spread_h) + placed(spread_l), axis=0)
            ratio = jnp.dot(coef2, spread, preferred_element_type=F32)
            fre = meta[4:5] + meta[5:6]
            fim = meta[6:7] + meta[7:8]
            re = fre * ratio[:half] - fim * ratio[half:]
            im = fre * ratio[half:] + fim * ratio[:half]
            at = r * count
            dens[0:half, at : at + count] = re.astype(BF16)
            dens[half:fields2, at : at + count] = im.astype(BF16)
            at = (rounds + r) * count
            dens[0:half, at : at + count] = (-im).astype(BF16)
            dens[half:fields2, at : at + count] = re.astype(BF16)

    kerns = (kern0, kern1, kern2)
    tile = (rows + 16) // 3
    width = rounds * count

    def apply(saug, dens):
        for m in range(3):
            kern = kerns[m]
            square = jnp.dot(
                taug[m * tile : (m + 1) * tile, :], saug[...], preferred_element_type=F32
            )
            for i in range(0, tile, 16):
                re, im = wave_terms(square[i : i + 16])
                kern[i : i + 16, 0:width] = re.astype(BF16)
                kern[i : i + 16, width : 2 * width] = im.astype(BF16)
            acc[m * tile : (m + 1) * tile, :] += lax.dot_general(
                kern[...], dens[...], (((1,), (1,)), ((), ())), preferred_element_type=F32
            )

    prepare(0, saug_a, dens_a)

    def pair(q, carry):
        slot = 2 * q
        forward(slot).wait_recv()
        prepare(slot + 1, saug_b, dens_b)
        apply(saug_a, dens_a)

        @pl.when(q < n_tgt // 2 - 1)
        def _():
            direct_recv(slot + 2).wait_recv()
            forward(slot + 2).start()
            prepare(slot + 2, saug_a, dens_a)

        apply(saug_b, dens_b)
        return carry

    def direct_recv(slot):
        return pltpu.make_async_remote_copy(
            src_ref=gather.at[0],
            dst_ref=gather.at[slot],
            send_sem=send_sem.at[slot],
            recv_sem=recv_sem.at[slot],
            device_id=(flip(me, 1), sme),
            device_id_type=MESH,
        )

    lax.fori_loop(0, n_tgt // 2, pair, 0)

    def share(bits, m):
        return pltpu.make_async_remote_copy(
            src_ref=part.at[pl.ds(m * tile, tile)],
            dst_ref=peers.at[bits, pl.ds(m * tile, tile)],
            send_sem=psend.at[bits, m],
            recv_sem=precv.at[bits, m],
            device_id=(me, flip(sme, bits)),
            device_id_type=MESH,
        )

    for m in range(3):
        part[m * tile : (m + 1) * tile, :] = acc[m * tile : (m + 1) * tile, :].astype(BF16)
        for bits in range(1, n_src):
            share(bits, m).start()

    for m in range(3):
        at = slice(m * tile, (m + 1) * tile)
        for bits in range(1, n_src):
            share(bits, m).wait_recv()
        terms = [part[at, :].astype(F32)]
        terms += [peers[bits, at, :].astype(F32) for bits in range(1, n_src)]
        while len(terms) > 1:
            terms = [terms[k] + terms[k + 1] for k in range(0, len(terms), 2)]
        acc[at, :] = terms[0] * scale

    pot[HALO : HALO + rows, :] = acc[0:rows, :] * bw[:, 8:9]
    pot[HALO + rows : HALO + rows + 8, :] = acc[rows : rows + 8, :] * hw[0:8, 3:4]
    pot[0:HALO, :] = acc[rows + 8 : rows + 16, :] * hw[8:16, 3:4]
    for start in range(0, rows, 128):
        value = pot[HALO + start : HALO + start + 128, :]
        for d in range(band_ref.shape[0]):
            shifted = pot[pl.ds(HALO + start + off_ref[d], 128), :]
            value = value + bw[start : start + 128, d : d + 1] * shifted
        out_ref[start : start + 128, :] = value

    for bits in range(1, n_tgt):
        direct_recv(bits).wait_send()
    for m in range(3):
        for bits in range(1, n_src):
            share(bits, m).wait_send()


def per_device(n_tgt, n_src, tgt_points, tgt_weight, src_points, src_weight, basis, span,
               patch, patch_factor, ctrl_weight, ctrl_coef, band, offsets):
    rows = tgt_points.shape[1]
    rounds, fields2, ctrl = ctrl_coef.shape
    count = src_weight.shape[1]
    sources = rounds * count * n_tgt * n_src
    scale = OMEGA / math.sqrt(sources)
    total = rows + 16
    width = rounds * count
    vmem = pl.BlockSpec(memory_space=pltpu.VMEM)
    smem = pl.BlockSpec(memory_space=pltpu.SMEM)
    return pl.pallas_call(
        functools.partial(body, n_tgt, n_src, scale),
        out_shape=jax.ShapeDtypeStruct((rows, fields2), F32),
        in_specs=[vmem] * 7 + [smem, smem, vmem, vmem, smem],
        out_specs=vmem,
        scratch_shapes=[
            pltpu.VMEM((n_tgt, fields2 + 16 * rounds, rounds * ctrl), BF16),
            pltpu.VMEM((total, 16), BF16),
            pltpu.VMEM((rows, 16), F32),
            pltpu.VMEM((2, 8, 128), F32),
            pltpu.VMEM((2, 8, 128), F32),
            pltpu.VMEM((16, 8), F32),
            pltpu.VMEM((16, width), BF16),
            pltpu.VMEM((16, width), BF16),
            pltpu.VMEM((fields2, 2 * width), BF16),
            pltpu.VMEM((fields2, 2 * width), BF16),
            pltpu.VMEM((total // 3, 2 * width), BF16),
            pltpu.VMEM((total // 3, 2 * width), BF16),
            pltpu.VMEM((total // 3, 2 * width), BF16),
            pltpu.VMEM((total, fields2), F32),
            pltpu.VMEM((total, fields2), BF16),
            pltpu.VMEM((n_src, total, fields2), BF16),
            pltpu.VMEM((total, fields2), F32),
            pltpu.SemaphoreType.DMA((n_tgt,)),
            pltpu.SemaphoreType.DMA((n_tgt,)),
            pltpu.SemaphoreType.DMA((2,)),
            pltpu.SemaphoreType.DMA((2,)),
            pltpu.SemaphoreType.DMA((n_src, 3)),
            pltpu.SemaphoreType.DMA((n_src, 3)),
        ],
        compiler_params=pltpu.CompilerParams(
            collective_id=0, has_side_effects=True, vmem_limit_bytes=40 * 1024 * 1024
        ),
    )(
        tgt_points,
        tgt_weight.reshape(1, rows),
        src_points,
        src_weight,
        basis,
        span,
        patch,
        patch_factor,
        ctrl_weight,
        ctrl_coef,
        band,
        offsets,
    )


def solution(mesh):
    in_specs = (
        P(None, "tgt"),
        P("tgt"),
        P(None, None, ("tgt", "src")),
        P(None, ("tgt", "src")),
        P(None, None, ("tgt", "src")),
        P(None, ("tgt", "src")),
        P(None, ("tgt", "src")),
        P(None, None, ("tgt", "src")),
        P(None, ("tgt", "src")),
        P(None, None, ("tgt", "src")),
        P(None, "tgt"),
        P(),
    )
    return jax.shard_map(
        functools.partial(per_device, mesh.shape["tgt"], mesh.shape["src"]),
        mesh=mesh,
        in_specs=in_specs,
        out_specs=P("tgt", None),
        check_vma=False,
    )
```

```python
import functools
import math

import jax
import jax.numpy as jnp
from jax import lax
from jax.experimental import pallas as pl
from jax.experimental.pallas import tpu as pltpu
from jax.sharding import PartitionSpec as P

HALO = 8
WAVE = 8.0
SMOOTH = 0.0025
OMEGA = WAVE / (2.0 * math.pi)
KAPPA = OMEGA * OMEGA
MAGIC = 12582912.0

F32 = jnp.float32
BF16 = jnp.bfloat16
MESH = pl.DeviceIdType.MESH


def pieces(value):
    high = value.astype(BF16).astype(F32)
    rest = value - high
    mid = rest.astype(BF16).astype(F32)
    return high, mid, (rest - mid).astype(BF16).astype(F32)


def flip(index, bits):
    out = index
    place = 1
    while place <= bits:
        if bits // place % 2:
            out = out + (1 - 2 * ((index // place) % 2)) * place
        place *= 2
    return out


def target_rows(points):
    square = KAPPA * (
        points[0:1] * points[0:1] + points[1:2] * points[1:2] + points[2:3] * points[2:3]
    )
    high, mid, low = pieces(square)
    one = jnp.ones_like(square)
    return jnp.concatenate(
        [points, points, points, high, mid, low, one, one, one, jnp.zeros_like(one)], axis=0
    )


def source_rows(points):
    square = KAPPA * (
        SMOOTH
        + points[0:1] * points[0:1]
        + points[1:2] * points[1:2]
        + points[2:3] * points[2:3]
    )
    high, mid, low = pieces(square)
    ph, pm, plo = pieces(points * (-2.0 * KAPPA))
    one = jnp.ones_like(square)
    return jnp.concatenate(
        [ph, pm, plo, one, one, one, high, mid, low, jnp.zeros_like(one)], axis=0
    )


SIN = (4.441527135827024, -7.264541902232219, 3.2516001820136307)
COS = (1.4133599520203266, -6.916869803046874, 5.067054327781224)


def wave_terms(square):
    inv = lax.rsqrt(square)
    turns = square * inv
    frac = turns - ((turns + MAGIC) - MAGIC)
    z = frac * frac
    half_sin = frac * (SIN[0] + z * (SIN[1] + z * SIN[2]))
    half_cos = COS[0] + z * (COS[1] + z * COS[2])
    prod = half_sin * inv
    return inv - half_sin * prod, prod * half_cos


def body(
    n_tgt,
    n_src,
    scale,
    tgt_ref,
    tw_ref,
    src_ref,
    sw_ref,
    basis_ref,
    span_ref,
    patch_ref,
    pf_ref,
    cw_ref,
    coef_ref,
    band_ref,
    off_ref,
    out_ref,
    gather,
    taug,
    bw,
    hal_own,
    hal_in,
    hw,
    saug,
    dens,
    kern0,
    kern1,
    kern2,
    kern3,
    kern4,
    kern5,
    acc,
    part,
    peers,
    pot,
    send_sem,
    recv_sem,
    fsem,
    gsem,
    hsend,
    hrecv,
    psend,
    precv,
):
    me = lax.axis_index("tgt")
    sme = lax.axis_index("src")
    rows = tgt_ref.shape[1]
    rounds, ctrl, fields2 = coef_ref.shape
    half = fields2 // 2
    count = sw_ref.shape[1]
    base = rounds * ctrl
    width = rounds * count
    odd = me % 2
    up = (me + 1) % n_tgt
    down = (me + n_tgt - 1) % n_tgt
    other = (me + n_tgt - 1 + 2 * odd) % n_tgt

    barrier = pltpu.get_barrier_semaphore()
    greeted = 0
    for bits in [1] + list(range(2, n_tgt, 2)):
        pl.semaphore_signal(
            barrier, inc=1, device_id=(flip(me, bits), sme), device_id_type=MESH
        )
        greeted += 1
    pl.semaphore_signal(barrier, inc=1, device_id=(other, sme), device_id_type=MESH)
    greeted += 1
    for bits in range(1, n_src):
        pl.semaphore_signal(
            barrier, inc=1, device_id=(me, flip(sme, bits)), device_id_type=MESH
        )
        greeted += 1

    for r in range(rounds):
        gather[0, ctrl * r : ctrl * (r + 1), :] = coef_ref[r]
        span = span_ref[r : r + 1, :]
        index = jnp.broadcast_to(span, (8, count)) + lax.broadcasted_iota(
            jnp.int32, (8, count), 0
        )
        weights = jnp.zeros((8, count), F32)
        for c in range(ctrl):
            weights = jnp.where(index == c, cw_ref[r, c], weights)
        scaled = basis_ref[r] * weights[0:3]
        denom = scaled[0:1] + scaled[1:2] + scaled[2:3]
        scaled = scaled * (sw_ref[r : r + 1, :] / denom)
        patch = patch_ref[r : r + 1, :]
        fre = jnp.zeros((1, count), F32)
        fim = jnp.zeros((1, count), F32)
        for p in range(pf_ref.shape[2]):
            fre = jnp.where(patch == p, pf_ref[r, 0, p], fre)
            fim = jnp.where(patch == p, pf_ref[r, 1, p], fim)
        rh, rl, _ = pieces(scaled * fre)
        ih, il, _ = pieces(scaled * fim)
        meta = jnp.concatenate(
            [src_ref[r].astype(F32), span.astype(F32), rh, rl, ih, il], axis=0
        )
        gather[0, base + 16 * r : base + 16 * (r + 1), :] = meta.astype(BF16)

    points = tgt_ref[...].astype(F32)
    tweight = tw_ref[...]
    strip = jnp.concatenate([points, tweight, jnp.zeros((4, rows), F32)], axis=0)
    hal_own[0] = strip[:, 0:128]
    hal_own[1] = strip[:, rows - 128 : rows]

    pl.semaphore_wait(barrier, greeted)

    def direct(bits):
        return pltpu.make_async_remote_copy(
            src_ref=gather.at[0],
            dst_ref=gather.at[bits],
            send_sem=send_sem.at[bits],
            recv_sem=recv_sem.at[bits],
            device_id=(flip(me, bits), sme),
            device_id_type=MESH,
        )

    def forward(slot):
        return [
            pltpu.make_async_remote_copy(
                src_ref=ref.at[slot],
                dst_ref=ref.at[slot + 1],
                send_sem=sems.at[0, slot // 2],
                recv_sem=sems.at[1, slot // 2],
                device_id=(flip(me, 1), sme),
                device_id_type=MESH,
            )
            for ref, sems in ((saug, fsem), (dens, gsem))
        ]

    def hand_on(slot):
        for copy in forward(slot):
            copy.start()

    def handed(slot):
        for copy in forward(slot):
            copy.wait_recv()

    for bits in range(2, n_tgt, 2):
        direct(bits).start()
    halo_up = pltpu.make_async_remote_copy(
        src_ref=hal_own.at[1],
        dst_ref=hal_in.at[0],
        send_sem=hsend.at[0],
        recv_sem=hrecv.at[0],
        device_id=(up, sme),
        device_id_type=MESH,
    )
    halo_down = pltpu.make_async_remote_copy(
        src_ref=hal_own.at[0],
        dst_ref=hal_in.at[1],
        send_sem=hsend.at[1],
        recv_sem=hrecv.at[1],
        device_id=(down, sme),
        device_id_type=MESH,
    )
    halo_up.start()
    halo_down.start()

    taug[0:rows, :] = jnp.transpose(target_rows(points)).astype(BF16)
    bw[...] = jnp.transpose(
        jnp.concatenate([band_ref[...], strip[3:4], jnp.zeros((7, rows), F32)], axis=0)
    )
    acc[...] = jnp.zeros_like(acc)
    halo_up.wait()
    halo_down.wait()
    low = hal_in[0]
    high = hal_in[1]
    low_t = jnp.transpose(target_rows(low[0:3]))
    high_t = jnp.transpose(target_rows(high[0:3]))
    taug[rows : rows + 16, :] = jnp.concatenate(
        [high_t[0:8], low_t[120:128]], axis=0
    ).astype(BF16)
    hw[0:8, :] = jnp.transpose(high)[0:8] * jnp.where(me < n_tgt - 1, 1.0, 0.0)
    hw[8:16, :] = jnp.transpose(low)[120:128] * jnp.where(me > 0, 1.0, 0.0)

    lane = lax.broadcasted_iota(jnp.int32, (1, fields2), 1)
    sign = jnp.where(lane < half, -1.0, 1.0)

    def turned(value):
        return pltpu.roll(value, half, 1) * sign

    def prepare(source, slot):
        coef = gather[source, 0:base, :]
        coef_i = turned(coef.astype(F32)).astype(BF16)
        label = lax.broadcasted_iota(jnp.int32, (ctrl, count), 0).astype(F32)
        for r in range(rounds):
            meta = gather[source, base + 16 * r : base + 16 * (r + 1), :].astype(F32)
            saug[slot, :, r * count : (r + 1) * count] = source_rows(meta[0:3]).astype(BF16)
            hits = [label == meta[3:4] + float(a) for a in range(3)]
            blocks = []
            for kind in range(4):
                block = jnp.zeros((ctrl, count), F32)
                for a in range(3):
                    row = 4 + 3 * kind + a
                    block = jnp.where(hits[a], meta[row : row + 1], block)
                blocks.append(block)
            spread = jnp.transpose(jnp.concatenate(blocks, axis=0)).astype(BF16)
            part_r = coef[ctrl * r : ctrl * (r + 1)]
            part_i = coef_i[ctrl * r : ctrl * (r + 1)]
            values = jnp.dot(
                spread,
                jnp.concatenate([part_r, part_r, part_i, part_i], axis=0),
                preferred_element_type=F32,
            )
            dens[slot, r * count : (r + 1) * count, :] = values.astype(BF16)

    tile = (rows + 16) // 3
    kerns = (kern0, kern1, kern2, kern3, kern4, kern5)

    def apply(first, blocks, m):
        kre, kim = kerns[2 * m], kerns[2 * m + 1]
        at = slice(m * tile, (m + 1) * tile)
        for j in range(blocks):
            square = jnp.dot(taug[at, :], saug[first + j], preferred_element_type=F32)
            columns = slice(j * width, (j + 1) * width)
            for i in range(0, tile, 16):
                re, im = wave_terms(square[i : i + 16])
                kre[i : i + 16, columns] = re.astype(BF16)
                kim[i : i + 16, columns] = im.astype(BF16)
        columns = slice(0, blocks * width)
        held = dens[pl.ds(first, blocks)].reshape(blocks * width, fields2)
        acc[at, 0:fields2] += jnp.dot(kre[:, columns], held, preferred_element_type=F32)
        acc[at, fields2:] += jnp.dot(kim[:, columns], held, preferred_element_type=F32)

    def arrived(slot):
        return pltpu.make_async_remote_copy(
            src_ref=gather.at[0],
            dst_ref=gather.at[slot],
            send_sem=send_sem.at[slot],
            recv_sem=recv_sem.at[slot],
            device_id=(flip(me, 2), sme),
            device_id_type=MESH,
        )

    prepare(0, 0)
    hand_on(0)
    for m in range(3):
        apply(0, 1, m)
    arrived(2).wait_recv()
    prepare(2, 2)
    hand_on(2)

    def step(q, carry):
        arrived(2 * q + 2).wait_recv()
        handed(2 * q - 2)
        prepare(2 * q + 2, 2 * q + 2)
        for m in range(3):
            apply(2 * q - 1, 2, m)
        hand_on(2 * q + 2)
        return carry

    lax.fori_loop(1, n_tgt // 2 - 1, step, 0)

    def share(bits, m):
        return pltpu.make_async_remote_copy(
            src_ref=part.at[pl.ds(m * tile, tile)],
            dst_ref=peers.at[bits, pl.ds(m * tile, tile)],
            send_sem=psend.at[bits, m],
            recv_sem=precv.at[bits, m],
            device_id=(me, flip(sme, bits)),
            device_id_type=MESH,
        )

    handed(n_tgt - 4)
    for m in range(3):
        at = slice(m * tile, (m + 1) * tile)
        apply(n_tgt - 3, 2, m)
        if m == 0:
            handed(n_tgt - 2)
        apply(n_tgt - 1, 1, m)
        part[at, :] = (acc[at, 0:fields2] + turned(acc[at, fields2:])).astype(BF16)
        for bits in range(1, n_src):
            share(bits, m).start()

    for m in range(3):
        at = slice(m * tile, (m + 1) * tile)
        for bits in range(1, n_src):
            share(bits, m).wait_recv()
        terms = [part[at, :].astype(F32)]
        terms += [peers[bits, at, :].astype(F32) for bits in range(1, n_src)]
        while len(terms) > 1:
            terms = [terms[k] + terms[k + 1] for k in range(0, len(terms), 2)]
        acc[at, 0:fields2] = terms[0] * scale

    pot[HALO : HALO + rows, :] = acc[0:rows, 0:fields2] * bw[:, 8:9]
    pot[HALO + rows : HALO + rows + 8, :] = acc[rows : rows + 8, 0:fields2] * hw[0:8, 3:4]
    pot[0:HALO, :] = acc[rows + 8 : rows + 16, 0:fields2] * hw[8:16, 3:4]
    for start in range(0, rows, 128):
        value = pot[HALO + start : HALO + start + 128, :]
        for d in range(band_ref.shape[0]):
            shifted = pot[pl.ds(HALO + start + off_ref[d], 128), :]
            value = value + bw[start : start + 128, d : d + 1] * shifted
        out_ref[start : start + 128, :] = value

    for bits in range(2, n_tgt, 2):
        direct(bits).wait_send()
    for slot in range(0, n_tgt, 2):
        for copy in forward(slot):
            copy.wait_send()
    for m in range(3):
        for bits in range(1, n_src):
            share(bits, m).wait_send()


def per_device(n_tgt, n_src, tgt_points, tgt_weight, src_points, src_weight, basis, span,
               patch, patch_factor, ctrl_weight, ctrl_coef, band, offsets):
    rows = tgt_points.shape[1]
    rounds, fields2, ctrl = ctrl_coef.shape
    count = src_weight.shape[1]
    sources = rounds * count * n_tgt * n_src
    scale = OMEGA / math.sqrt(sources)
    total = rows + 16
    width = rounds * count
    vmem = pl.BlockSpec(memory_space=pltpu.VMEM)
    smem = pl.BlockSpec(memory_space=pltpu.SMEM)
    return pl.pallas_call(
        functools.partial(body, n_tgt, n_src, scale),
        out_shape=jax.ShapeDtypeStruct((rows, fields2), F32),
        in_specs=[vmem] * 7 + [smem, smem, vmem, vmem, smem],
        out_specs=vmem,
        scratch_shapes=[
            pltpu.VMEM((n_tgt, rounds * (ctrl + 16), fields2), BF16),
            pltpu.VMEM((total, 16), BF16),
            pltpu.VMEM((rows, 16), F32),
            pltpu.VMEM((2, 8, 128), F32),
            pltpu.VMEM((2, 8, 128), F32),
            pltpu.VMEM((16, 8), F32),
            pltpu.VMEM((n_tgt, 16, width), BF16),
            pltpu.VMEM((n_tgt, width, fields2), BF16),
            pltpu.VMEM((total // 3, 2 * width), BF16),
            pltpu.VMEM((total // 3, 2 * width), BF16),
            pltpu.VMEM((total // 3, 2 * width), BF16),
            pltpu.VMEM((total // 3, 2 * width), BF16),
            pltpu.VMEM((total // 3, 2 * width), BF16),
            pltpu.VMEM((total // 3, 2 * width), BF16),
            pltpu.VMEM((total, 2 * fields2), F32),
            pltpu.VMEM((total, fields2), BF16),
            pltpu.VMEM((n_src, total, fields2), BF16),
            pltpu.VMEM((total, fields2), F32),
            pltpu.SemaphoreType.DMA((n_tgt,)),
            pltpu.SemaphoreType.DMA((n_tgt,)),
            pltpu.SemaphoreType.DMA((2, n_tgt // 2)),
            pltpu.SemaphoreType.DMA((2, n_tgt // 2)),
            pltpu.SemaphoreType.DMA((2,)),
            pltpu.SemaphoreType.DMA((2,)),
            pltpu.SemaphoreType.DMA((n_src, 3)),
            pltpu.SemaphoreType.DMA((n_src, 3)),
        ],
        compiler_params=pltpu.CompilerParams(
            collective_id=0, has_side_effects=True, vmem_limit_bytes=40 * 1024 * 1024
        ),
    )(
        tgt_points,
        tgt_weight.reshape(1, rows),
        src_points,
        src_weight,
        basis,
        span,
        patch,
        patch_factor,
        ctrl_weight,
        jnp.transpose(ctrl_coef, (0, 2, 1)),
        band,
        offsets,
    )


def solution(mesh):
    in_specs = (
        P(None, "tgt"),
        P("tgt"),
        P(None, None, ("tgt", "src")),
        P(None, ("tgt", "src")),
        P(None, None, ("tgt", "src")),
        P(None, ("tgt", "src")),
        P(None, ("tgt", "src")),
        P(None, None, ("tgt", "src")),
        P(None, ("tgt", "src")),
        P(None, None, ("tgt", "src")),
        P(None, "tgt"),
        P(),
    )
    return jax.shard_map(
        functools.partial(per_device, mesh.shape["tgt"], mesh.shape["src"]),
        mesh=mesh,
        in_specs=in_specs,
        out_specs=P("tgt", None),
        check_vma=False,
    )
```
